1024 devices in a mesh: row: 32 (over z, y_hi, core), col: 32 (over y_lo, x).
Axes of the slice: x: 8, y: 8 (y_hi: 2, y_lo: 4; y = y_hi * 4 + y_lo), z: 8, core: 2. Of those that a mesh axis runs over, the one named last changes fastest.
Arguments:
- grad: bfloat16 [8192, 4096], P('row', 'col'), may hold values from -6 to 6
- basis_t: bfloat16 [8192, 8192], P('row', 'col'), may hold values from -0.125 to 0.125
- first_moment: float32 [8192, 4096], P('row', 'col'), may hold values from -4 to 4
- second_moment: float32 [8192, 4096], P('row', 'col'), may hold values from 0.1 to 3
- master: float32 [8192, 4096], P('row', 'col'), may hold values from -6 to 6
Outputs:
- new_first: float32 [8192, 4096], P('row', 'col')
- new_second: float32 [8192, 4096], P('row', 'col')
- new_master: float32 [8192, 4096], P('row', 'col')
- new_weight: bfloat16 [8192, 4096], P('row', 'col')
- rotated_back: float32 [8192, 4096], P('row', 'col')
The draws below stay inside these ranges and needn't reach their ends.
All inputs are finite; a program needn't handle non-finite values.
Results may differ from the reference program's by a relative error of at most 0.019.
Values may be sent and summed in bfloat16 or wider, within the bound.
A program may use at most 32 MiB of HBM per device.

```python
import math
import jax
import jax.numpy as jnp
from jax import lax

DM = 8192
COLS = 4096
STEP = 10
N_ROW = 32


def raised(values, rng, source, target, blocks, factor):
    owner, partner = [(jnp.arange(values.shape[axis_at]) // (values.shape[axis_at] // blocks)).reshape([-1 if axis == axis_at else 1 for axis in range(values.ndim)]) for axis_at in (source, target)]
    chosen = jax.random.permutation(rng, blocks)[partner]
    strong = (owner == chosen) | (owner == (partner + blocks // 2) % blocks)
    return jnp.where(strong, factor * values, values)


def steps_of(own_key, extent, pieces, least, high):
    factor_of = 1.0
    for axis_at, parts in pieces:
        steps = jax.random.uniform(jax.random.fold_in(jax.random.fold_in(own_key, 6), axis_at), (parts,), jnp.float32, least / len(pieces), high / len(pieces))
        factor_of = factor_of * jnp.repeat(jnp.exp(steps), extent[axis_at] // parts).reshape((-1,) + (1,) * (len(extent) - 1 - axis_at))
    return factor_of


def bell_draw(rng, extent, spread, most, shards=(), held_as=jnp.bfloat16):
    gain = steps_of(rng, extent, shards, -0.22, 0.18) if shards else 1.0
    result = jax.random.normal(rng, extent, jnp.float32) * spread * gain
    return jnp.minimum(jnp.maximum(result, -most), most).astype(held_as)


def heavy_noise(own_key, extent, width, most, cuts, heavy, held_as=jnp.bfloat16):
    values = width * jax.random.normal(own_key, extent, jnp.float32)
    if cuts:
        values = values * steps_of(own_key, extent, cuts, -0.22, 0.18)
    return jnp.clip(raised(values, jax.random.fold_in(own_key, 3), *heavy), -most, most).astype(held_as)


def setup_inputs(seed: int = 0) -> dict:
    arg_keys = jax.random.split(jax.random.key(seed), 6)
    grad = bell_draw(arg_keys[0], (DM, COLS), 1.0, 6.0, ((0, 32), (1, 32)))
    basis_t = heavy_noise(arg_keys[1], (DM, DM), DM ** -0.5, 0.125, ((0, 32), (1, 32)), (0, 1, 32, 2.75))
    first_moment = bell_draw(arg_keys[2], (DM, COLS), 0.5, 4.0, ((0, 32), (1, 32)), jnp.float32)
    second_moment = jnp.clip(jnp.exp(math.log(3.0) - 3.4011974 * jax.random.uniform(arg_keys[3], (DM, COLS), jnp.float32) ** steps_of(arg_keys[3], (DM, COLS), ((0, 32), (1, 32)), -0.2, 0.2)), 0.1, 3.0)
    master = bell_draw(arg_keys[4], (DM, COLS), 1.0, 6.0, ((0, 32), (1, 32)), jnp.float32)
    return {"grad": grad, "basis_t": basis_t, "first_moment": first_moment, "second_moment": second_moment, "master": master}


BETA_ONE = 0.9
BETA_TWO = 0.95
EPSILON = 1e-08
LEARN = 0.01
DECAY = 0.1

def reference(grad, basis_t, first_moment, second_moment, master):
    rotated = jnp.dot(basis_t, grad, preferred_element_type=jnp.float32)
    new_first = BETA_ONE * first_moment + (1.0 - BETA_ONE) * rotated
    new_second = BETA_TWO * second_moment + (1.0 - BETA_TWO) * rotated * rotated
    corr_one = 1.0 - BETA_ONE ** STEP
    corr_two = 1.0 - BETA_TWO ** STEP
    direction = (new_first / corr_one / (jnp.sqrt(new_second / corr_two) + EPSILON)).astype(jnp.bfloat16)
    block_rows = DM // N_ROW
    basis_blocks = basis_t.reshape(N_ROW, block_rows, DM)
    direction_blocks = direction.reshape(N_ROW, block_rows, COLS)

    def add_block(total, pair):
        basis_block, direction_block = pair
        partial_value = lax.dot_general(basis_block, direction_block, (((0,), (0,)), ((), ())), preferred_element_type=jnp.float32)
        rounded = lax.optimization_barrier(partial_value.astype(jnp.bfloat16))
        return (total + rounded.astype(jnp.float32), None)
    rotated_back, unused = lax.scan(add_block, jnp.zeros((DM, COLS), jnp.float32), (basis_blocks, direction_blocks))
    new_master = master * (1.0 - LEARN * DECAY) - LEARN * rotated_back
    new_weight = new_master.astype(jnp.bfloat16)
    return (new_first, new_second, new_master, new_weight, rotated_back)
```

```python
import jax
import jax.numpy as jnp
from jax import lax
from jax.experimental import pallas as pl
from jax.experimental.pallas import tpu as pltpu
from jax.sharding import PartitionSpec as P

STEP = 10
BETA_ONE = 0.9
BETA_TWO = 0.95
EPSILON = 1e-08
LEARN = 0.01
DECAY = 0.1

MESH = pl.DeviceIdType.MESH
F32 = jnp.float32
BF16 = jnp.bfloat16

RIGHT = (4, 3, 3, 4)
LEFT = (3, 4, 4, 3)
Z_RIGHT = (4, 3)
Z_LEFT = (3, 4)
DELTAS = (4, 3, -3, 2, -2, 1, -1, 0)


def kernel(
    g_ref, b_ref, fm_ref, sm_ref, ma_ref,
    nf_ref, ns_ref, nm_ref, nw_ref, rb_ref,
    stage, wide, tall, acc, part_out, part_in, turned,
    own, core_out, core_in, ring_out, ring_in, last_out, last_in,
    y_s, y_r, x_s, x_r, g_s, g_r, z_s, z_r, gc_s, gc_r, p_s, p_r, tc_s, tc_r, r_s, r_r, f_s, f_r,
):
    row, col = lax.axis_index("row"), lax.axis_index("col")
    z, yh, c = row // 4, (row // 2) % 2, row % 2
    yl, x = col // 8, col % 8
    h = yl % 2
    mate = yl + 1 - 2 * h
    far = 1 - yh

    def at(z_, yh_, c_, yl_, x_):
        return (z_ * 4 + yh_ * 2 + c_, yl_ * 8 + x_)

    right, left = at(z, yh, c, yl, (x + 1) % 8), at(z, yh, c, yl, (x + 7) % 8)
    above, below = at((z + 1) % 8, yh, c, yl, x), at((z + 7) % 8, yh, c, yl, x)
    twin = at(z, yh, 1 - c, yl, x)
    pair = at(z, yh, c, mate, x)
    across = at(z, far, c, yl, x)
    across_pair = at(z, far, c, mate, x)

    waits = []

    def copy(src, dst, send, recv, to):
        made = pltpu.make_async_remote_copy(
            src_ref=src, dst_ref=dst, send_sem=send, recv_sem=recv, device_id=to, device_id_type=MESH
        )
        made.start()
        waits.append(made)

    def arrived(dst, send, recv, frm):
        pltpu.make_async_remote_copy(
            src_ref=dst, dst_ref=dst, send_sem=send, recv_sem=recv, device_id=frm, device_id_type=MESH
        ).wait_recv()

    here = yl * 8 + x
    stage[0] = b_ref[:, 0:128]
    stage[1] = b_ref[:, 128:256]
    wide[here] = stage[h]
    tall[z, c, yh, 0] = g_ref[pl.ds(pl.multiple_of(h * 128, 128), 128), :]

    barrier = pltpu.get_barrier_semaphore()
    peers = [right, left, above, below, twin, across, across_pair]
    peers += [at(z, yh, c, (yl + d) % 4, x) for d in (1, 2, 3)]
    for peer in peers:
        pl.semaphore_signal(barrier, inc=1, device_id=peer, device_id_type=MESH)
    pl.semaphore_wait(barrier, len(peers))

    def x_step(d, s):
        line = ((yl + 4 - d) % 4) * 8
        for way, count, sign, to in ((0, RIGHT[d], -1, right), (1, LEFT[d], 1, left)):
            if s >= count:
                continue
            slot = wide.at[line + (x + 8 + sign * s) % 8]
            if s:
                arrived(slot, x_s.at[way, d, s - 1], x_r.at[way, d, s - 1], to)
            copy(slot, slot, x_s.at[way, d, s], x_r.at[way, d, s], to)

    def x_last(d, way):
        line = ((yl + 4 - d) % 4) * 8
        count, sign, to = ((RIGHT[d], -1, right), (LEFT[d], 1, left))[way]
        slot = wide.at[line + (x + 8 + sign * count) % 8]
        arrived(slot, x_s.at[way, d, count - 1], x_r.at[way, d, count - 1], to)

    def y_arrived(d):
        arrived(wide.at[((yl + 4 - d) % 4) * 8 + x], y_s.at[d - 1], y_r.at[d - 1], pair)

    halves = (yh, far)

    def to_twin(a, way, s):
        sign = (-1, 1)[way]
        slot = tall.at[(z + 8 + sign * s) % 8, c, halves[a]]
        copy(slot, slot, gc_s.at[way, a, s], gc_r.at[way, a, s], twin)

    def twin_arrived(a, way, s):
        sign = (-1, 1)[way]
        slot = tall.at[(z + 8 + sign * s) % 8, 1 - c, halves[a]]
        arrived(slot, gc_s.at[way, a, s], gc_r.at[way, a, s], twin)

    def z_step(a, s):
        for way, count, sign, to in ((0, Z_RIGHT[a], -1, above), (1, Z_LEFT[a], 1, below)):
            if s > count:
                continue
            slot = tall.at[(z + 8 + sign * s) % 8, c, halves[a]]
            if s:
                arrived(slot, z_s.at[way, a, s - 1], z_r.at[way, a, s - 1], to)
            if s < count:
                copy(slot, slot, z_s.at[way, a, s], z_r.at[way, a, s], to)
            if s or way == 0:
                to_twin(a, way, s)

    x_step(0, 0)
    keep = g_ref.at[pl.ds(pl.multiple_of(h * 128, 128), 128), :]
    give = g_ref.at[pl.ds(pl.multiple_of((1 - h) * 128, 128), 128), :]
    copy(give, tall.at[z, c, yh, 1], g_s.at[1], g_r.at[1], pair)
    copy(keep, tall.at[z, c, yh, 0], g_s.at[0], g_r.at[0], across)
    copy(give, tall.at[z, c, yh, 1], g_s.at[2], g_r.at[2], across_pair)
    for d in (1, 3, 2):
        there = (yl + d) % 4
        copy(stage.at[there % 2], wide.at[here], y_s.at[d - 1], y_r.at[d - 1], at(z, yh, c, there, x))

    arrived(tall.at[z, c, yh, 1], g_s.at[1], g_r.at[1], pair)
    z_step(0, 0)
    x_step(0, 1)
    y_arrived(1)
    x_step(1, 0)
    y_arrived(3)
    x_step(3, 0)
    arrived(tall.at[z, c, far, 0], g_s.at[0], g_r.at[0], across)
    arrived(tall.at[z, c, far, 1], g_s.at[2], g_r.at[2], across_pair)
    z_step(1, 0)
    z_step(0, 1)
    x_step(0, 2)
    y_arrived(2)
    x_step(2, 0)
    x_step(1, 1)
    x_step(3, 1)
    z_step(1, 1)
    z_step(0, 2)
    x_step(0, 3)
    x_step(2, 1)
    x_step(1, 2)
    x_step(3, 2)
    z_step(1, 2)
    z_step(0, 3)
    x_step(2, 2)
    x_step(1, 3)
    x_step(3, 3)
    z_step(1, 3)
    x_step(2, 3)
    z_step(0, 4)
    z_step(1, 4)
    for s in range(5):
        for a in (0, 1):
            for way, count in ((0, Z_RIGHT[a]), (1, Z_LEFT[a])):
                if s <= count and (s or way == 0):
                    twin_arrived(a, way, s)
    for d in range(4):
        x_last(d, 0 if RIGHT[d] == 3 else 1)

    def operands(delta):
        xs = (x + 8 + delta) % 8
        lhs = jnp.concatenate([wide[line * 8 + xs] for line in range(4)], axis=1)

        def rhs(e):
            return jnp.concatenate(
                [tall[line * 2 + xs // 4, xs % 2, (xs // 2) % 2, e] for line in range(4)], axis=0
            )

        return lhs, rhs

    for i, delta in enumerate((0, 1, -1, 2, -2, 3, -3)):
        lhs, rhs = operands(delta)
        for e in (0, 1):
            term = jnp.dot(lhs, rhs(e), preferred_element_type=F32)
            acc[e] = term if i == 0 else acc[e] + term
    for d in range(4):
        x_last(d, 0 if RIGHT[d] == 4 else 1)
    lhs, rhs = operands(4)
    part_out[...] = (acc[1] + jnp.dot(lhs, rhs(1), preferred_element_type=F32)).astype(BF16)
    copy(part_out, part_in, p_s.at[0], p_r.at[0], pair)
    acc[0] = acc[0] + jnp.dot(lhs, rhs(0), preferred_element_type=F32)
    arrived(part_in, p_s.at[0], p_r.at[0], pair)

    rotated = acc[0] + part_in[...].astype(F32)
    new_first = BETA_ONE * fm_ref[...] + (1.0 - BETA_ONE) * rotated
    new_second = BETA_TWO * sm_ref[...] + (1.0 - BETA_TWO) * rotated * rotated
    nf_ref[...] = new_first
    ns_ref[...] = new_second
    corr_one = 1.0 - BETA_ONE**STEP
    corr_two = 1.0 - BETA_TWO**STEP
    direction = new_first / corr_one / (jnp.sqrt(new_second / corr_two) + EPSILON)
    turned[0] = direction.T.astype(BF16)
    copy(turned.at[0], turned.at[1], p_s.at[1], p_r.at[1], pair)

    def terms(e):
        lhs = turned[e]
        for i, delta in enumerate(DELTAS):
            base = ((z + 8 + delta) % 8) * 4
            for half in (0, 1):
                rhs = jnp.concatenate([wide[base + half * 2 + c], wide[base + half * 2 + 1 - c]], axis=1)
                term = jnp.dot(lhs, rhs, preferred_element_type=F32)
                own[e, i, half] = term[:, 0:128]
                core_out[e, i, half] = term[:, 128:256].astype(BF16)
            copy(core_out.at[e, i], core_in.at[e, i], tc_s.at[e, i], tc_r.at[e, i], twin)

    def z_ring(e, t):
        for way, to in ((0, above), (1, below)):
            i = DELTAS.index((4 - t) if way == 0 or t == 0 else t - 4)
            if t or way == 0:
                arrived(core_in.at[e, i], tc_s.at[e, i], tc_r.at[e, i], twin)
            if t == 0:
                some = ring_out.at[way, e, 0, way]
                some[...] = (own[e, i, way] + core_in[e, i, way].astype(F32)).astype(BF16)
                copy(some, ring_in.at[way, e, 0, way], r_s.at[way, e, 0], r_r.at[way, e, 0], to)
                continue
            if t == 1:
                came = ring_in.at[way, e, 0, way]
                arrived(came, r_s.at[way, e, 0], r_r.at[way, e, 0], to)
                for half in (0, 1):
                    total = own[e, i, half] + core_in[e, i, half].astype(F32)
                    if half == way:
                        total += came[...].astype(F32)
                    ring_out[way, e, t, half] = total.astype(BF16)
            else:
                came = ring_in.at[way, e, t - 1]
                arrived(came, r_s.at[way, e, t - 1], r_r.at[way, e, t - 1], to)
                total = own[e, i] + core_in[e, i].astype(F32) + came[...].astype(F32)
                ring_out[way, e, t] = total.astype(BF16)
            copy(ring_out.at[way, e, t], ring_in.at[way, e, t], r_s.at[way, e, t], r_r.at[way, e, t], to)

    def z_sum(e):
        i = DELTAS.index(0)
        arrived(core_in.at[e, i], tc_s.at[e, i], tc_r.at[e, i], twin)
        for way, to in ((0, above), (1, below)):
            arrived(ring_in.at[way, e, 3], r_s.at[way, e, 3], r_r.at[way, e, 3], to)
        total = own[e, i] + core_in[e, i].astype(F32)
        total += ring_in[0, e, 3].astype(F32) + ring_in[1, e, 3].astype(F32)
        own[e, i] = total
        last_out[e] = total.astype(BF16)

    terms(0)
    z_ring(0, 0)
    arrived(turned.at[1], p_s.at[1], p_r.at[1], pair)
    terms(1)
    z_ring(1, 0)
    for t in (1, 2, 3):
        for e in (0, 1):
            z_ring(e, t)
    z_sum(0)
    copy(last_out.at[0, far], last_in.at[0], f_s.at[0], f_r.at[0], across)
    z_sum(1)
    copy(last_out.at[1, far], last_in.at[2], f_s.at[2], f_r.at[2], across_pair)
    copy(last_out.at[1, yh], last_in.at[1], f_s.at[1], f_r.at[1], pair)

    def finish(rows, value):
        back = value.T
        rb_ref[rows, :] = back
        new_master = ma_ref[rows, :] * (1.0 - LEARN * DECAY) - LEARN * back
        nm_ref[rows, :] = new_master
        nw_ref[rows, :] = new_master.astype(BF16)

    arrived(last_in.at[0], f_s.at[0], f_r.at[0], across)
    finish(
        pl.ds(pl.multiple_of(h * 128, 128), 128),
        own[0, DELTAS.index(0), yh] + last_in[0].astype(F32),
    )
    arrived(last_in.at[1], f_s.at[1], f_r.at[1], pair)
    arrived(last_in.at[2], f_s.at[2], f_r.at[2], across_pair)
    finish(
        pl.ds(pl.multiple_of((1 - h) * 128, 128), 128),
        last_in[1].astype(F32) + last_in[2].astype(F32),
    )
    for made in waits:
        made.wait_send()


def shards(grad, basis_t, first_moment, second_moment, master):
    rows, cols = grad.shape
    block = jax.ShapeDtypeStruct((rows, cols), F32)
    dma = pltpu.SemaphoreType.DMA
    return tuple(pl.pallas_call(
        kernel,
        out_shape=(block, block, block, jax.ShapeDtypeStruct((rows, cols), BF16), block),
        in_specs=[pl.BlockSpec(memory_space=pltpu.VMEM)] * 5,
        out_specs=tuple([pl.BlockSpec(memory_space=pltpu.VMEM)] * 5),
        scratch_shapes=[
            pltpu.VMEM((2, 256, 128), BF16),
            pltpu.VMEM((32, 256, 128), BF16),
            pltpu.VMEM((8, 2, 2, 2, 128, 128), BF16),
            pltpu.VMEM((2, 256, 128), F32),
            pltpu.VMEM((256, 128), BF16),
            pltpu.VMEM((256, 128), BF16),
            pltpu.VMEM((2, 128, 256), BF16),
            pltpu.VMEM((2, 8, 2, 128, 128), F32),
            pltpu.VMEM((2, 8, 2, 128, 128), BF16),
            pltpu.VMEM((2, 8, 2, 128, 128), BF16),
            pltpu.VMEM((2, 2, 4, 2, 128, 128), BF16),
            pltpu.VMEM((2, 2, 4, 2, 128, 128), BF16),
            pltpu.VMEM((2, 2, 128, 128), BF16),
            pltpu.VMEM((3, 128, 128), BF16),
            dma((3,)), dma((3,)),
            dma((2, 4, 4)), dma((2, 4, 4)),
            dma((3,)), dma((3,)),
            dma((2, 2, 4)), dma((2, 2, 4)),
            dma((2, 2, 5)), dma((2, 2, 5)),
            dma((2,)), dma((2,)),
            dma((2, 8)), dma((2, 8)),
            dma((2, 2, 4)), dma((2, 2, 4)),
            dma((3,)), dma((3,)),
        ],
        compiler_params=pltpu.CompilerParams(
            collective_id=0, has_side_effects=True, vmem_limit_bytes=40 * 2**20
        ),
        cost_estimate=pl.CostEstimate(flops=2 * 2 * 256 * 8192 * 128, bytes_accessed=2**20, transcendentals=0),
    )(grad, basis_t, first_moment, second_moment, master))


def solution(mesh):
    placed = tuple([P("row", "col")] * 5)
    return jax.shard_map(shards, mesh=mesh, in_specs=placed, out_specs=placed, check_vma=False)
```

```python
import jax
import jax.numpy as jnp
from jax import lax
from jax.experimental import pallas as pl
from jax.experimental.pallas import tpu as pltpu
from jax.sharding import PartitionSpec as P

STEP = 10
BETA_ONE = 0.9
BETA_TWO = 0.95
EPSILON = 1e-08
LEARN = 0.01
DECAY = 0.1

MESH = pl.DeviceIdType.MESH
F32 = jnp.float32
BF16 = jnp.bfloat16

Z_STEPS = (4, 3)
DELTAS = (4, 3, -3, 2, -2, 1, -1, 0)
HOME = DELTAS.index(0)


def kernel(
    g_ref, b_ref, fm_ref, sm_ref,
    rot_ref, near_ref, dist_ref,
    fm, sm, rot, near, dist, give, stage, wide, tall, acc, part_out, part_in, turned,
    own, core_out, core_in, ring_out, ring_in, last_out, last_in,
    l_s, w_s, y_s, y_r, x_s, x_r, g_s, g_r, z_s, z_r, gc_s, gc_r, p_s, p_r, tc_s, tc_r, r_s, r_r, f_s, f_r,
):
    row, col = lax.axis_index("row"), lax.axis_index("col")
    z, yh, c = row // 4, (row // 2) % 2, row % 2
    yl, x = col // 8, col % 8
    h = yl % 2
    mate = yl + 1 - 2 * h
    far = 1 - yh
    here = yl * 8 + x

    def at(z_, yh_, c_, yl_, x_):
        return (z_ * 4 + yh_ * 2 + c_, yl_ * 8 + x_)

    right, left = at(z, yh, c, yl, (x + 1) % 8), at(z, yh, c, yl, (x + 7) % 8)
    right2, left2 = at(z, yh, c, yl, (x + 2) % 8), at(z, yh, c, yl, (x + 6) % 8)
    above, below = at((z + 1) % 8, yh, c, yl, x), at((z + 7) % 8, yh, c, yl, x)
    above2, below2 = at((z + 2) % 8, yh, c, yl, x), at((z + 6) % 8, yh, c, yl, x)
    twin = at(z, yh, 1 - c, yl, x)
    pair = at(z, yh, c, mate, x)
    two_off = at(z, yh, c, (yl + 2) % 4, x)
    mirror = at(z, yh, c, 3 - yl, x)
    across = at(z, far, c, yl, x)
    across_pair = at(z, far, c, mate, x)

    mine = pl.ds(pl.multiple_of(h * 128, 128), 128)
    other = pl.ds(pl.multiple_of((1 - h) * 128, 128), 128)
    loads = [
        pltpu.make_async_copy(src, dst, l_s.at[i])
        for i, (src, dst) in enumerate((
            (b_ref.at[:, mine], wide.at[here]),
            (b_ref.at[:, other], stage),
            (g_ref.at[mine, :], tall.at[z, c, yh, 0]),
            (g_ref.at[other, :], give),
            (fm_ref, fm.at[0]), (sm_ref, sm.at[0]),
        ))
    ]
    for load in loads:
        load.start()
    barrier = pltpu.get_barrier_semaphore()
    peers = [right, left, right2, left2, above, below, above2, below2, twin, pair, two_off, mirror, across, across_pair]
    for peer in peers:
        pl.semaphore_signal(barrier, inc=1, device_id=peer, device_id_type=MESH)

    for load in loads[:4]:
        load.wait()
    pl.semaphore_wait(barrier, len(peers))

    waits = []

    def copy(src, dst, send, recv, to, later=True):
        made = pltpu.make_async_remote_copy(
            src_ref=src, dst_ref=dst, send_sem=send, recv_sem=recv, device_id=to, device_id_type=MESH
        )
        made.start()
        if later:
            waits.append(made)

    def arrived(dst, send, recv, frm):
        pltpu.make_async_remote_copy(
            src_ref=dst, dst_ref=dst, send_sem=send, recv_sem=recv, device_id=frm, device_id_type=MESH
        ).wait_recv()

    inner = ((yl + 1) // 2) % 2
    two, three = (yl + 2) % 4, 3 - yl
    lines = (yl, mate, inner * three + (1 - inner) * two, inner * two + (1 - inner) * three)
    came_by = (None, 0, inner + 1, 2 - inner)

    def x_slot(d, way, s):
        return wide.at[lines[d] * 8 + (x + 8 + (-1, 1)[way] * s) % 8]

    def x_half(d, way):
        return wide.at[lines[d] * 8 + (x + 4) % 8, pl.ds(way * 128, 128)]

    def x_step(d, s):
        for way, to in ((0, right), (1, left)):
            slot = x_slot(d, way, s)
            if s:
                arrived(slot, x_s.at[0], x_r.at[way, d, s - 1], to)
            if s == 3:
                slot = slot.at[pl.ds(way * 128, 128)]
            copy(slot, slot, x_s.at[0], x_r.at[way, d, s], to, later=False)

    def x_first():
        slot = x_slot(0, 0, 0)
        for s, ways in ((0, (right, left)), (1, (right2, left2))):
            for way in (0, 1):
                copy(slot, slot, x_s.at[0], x_r.at[way, 0, s], ways[way], later=False)

    def x_second():
        for way, one, two_on in ((0, right, right2), (1, left, left2)):
            slot = x_slot(0, way, 2)
            arrived(slot, x_s.at[0], x_r.at[way, 0, 1], one)
            copy(slot, slot, x_s.at[0], x_r.at[way, 0, 2], one, later=False)
            part = slot.at[pl.ds(way * 128, 128)]
            copy(part, part, x_s.at[0], x_r.at[way, 0, 3], two_on, later=False)

    def x_last(d):
        for way, one in ((0, right), (1, left)):
            if d == 0:
                arrived(x_slot(0, way, 1), x_s.at[0], x_r.at[way, 0, 0], one)
                arrived(x_slot(0, way, 3), x_s.at[0], x_r.at[way, 0, 2], one)
            arrived(x_half(d, way), x_s.at[0], x_r.at[way, d, 3], one)

    def y_step(d):
        arrived(wide.at[lines[d] * 8 + x], y_s.at[0], y_r.at[came_by[d]], pair)
        x_step(d, 0)

    halves = (yh, far)

    def to_twin(a, way, s):
        sign = (-1, 1)[way]
        slot = tall.at[(z + 8 + sign * s) % 8, c, halves[a]]
        copy(slot, slot, gc_s.at[0], gc_r.at[way, a, s], twin, later=False)

    def twin_arrived(a, way, s):
        sign = (-1, 1)[way]
        slot = tall.at[(z + 8 + sign * s) % 8, 1 - c, halves[a]]
        arrived(slot, gc_s.at[0], gc_r.at[way, a, s], twin)

    def z_step(s):
        for way, sign, to in ((0, -1, above), (1, 1, below)):
            if s > Z_STEPS[way]:
                continue
            slot = tall.at[(z + 8 + sign * s) % 8, c, yh]
            if s:
                arrived(slot, z_s.at[0], z_r.at[way, 0, s - 1], to)
            if s < Z_STEPS[way]:
                copy(slot, slot, z_s.at[0], z_r.at[way, 0, s], to, later=False)
            if s or way == 0:
                to_twin(0, way, s)

    def far_first():
        slot = tall.at[z, c, far]
        for s, ways in ((1, (above2, below2)), (0, (above, below))):
            for way in (0, 1):
                copy(slot, slot, z_s.at[0], z_r.at[way, 1, s], ways[way], later=False)
        to_twin(1, 0, 0)

    def far_second():
        for way, sign, one, two_on in ((0, -1, above, above2), (1, 1, below, below2)):
            slot = tall.at[(z + 8 + sign * 2) % 8, c, far]
            arrived(slot, z_s.at[0], z_r.at[way, 1, 1], one)
            copy(slot.at[way], slot.at[way], z_s.at[0], z_r.at[way, 1, 3], two_on, later=False)
            copy(slot, slot, z_s.at[0], z_r.at[way, 1, 2], one, later=False)
        for s in (2, 1):
            for way, sign, one in ((0, -1, above), (1, 1, below)):
                if s == 1:
                    arrived(tall.at[(z + 8 + sign) % 8, c, far], z_s.at[0], z_r.at[way, 1, 0], one)
                to_twin(1, way, s)

    def far_third():
        for way, sign, one in ((0, -1, above), (1, 1, below)):
            arrived(tall.at[(z + 8 + sign * 3) % 8, c, far], z_s.at[0], z_r.at[way, 1, 2], one)
            to_twin(1, way, 3)
        for way, one in ((0, above), (1, below)):
            arrived(tall.at[(z + 4) % 8, c, far, way], z_s.at[0], z_r.at[way, 1, 3], one)
        to_twin(1, 0, 4)

    x_first()
    copy(give, tall.at[z, c, yh, 1], g_s.at[1], g_r.at[1], pair)
    copy(stage, wide.at[here], y_s.at[0], y_r.at[0], pair)
    copy(tall.at[z, c, yh, 0], tall.at[z, c, yh, 0], g_s.at[0], g_r.at[0], across)
    copy(give, tall.at[z, c, yh, 1], g_s.at[2], g_r.at[2], across_pair)
    copy(stage, wide.at[here], y_s.at[2], y_r.at[2], mirror)
    copy(wide.at[here], wide.at[here], y_s.at[1], y_r.at[1], two_off)

    arrived(tall.at[z, c, yh, 1], g_s.at[1], g_r.at[1], pair)
    z_step(0)
    y_step(1)
    x_second()
    y_step(2)
    z_step(1)
    x_step(1, 1)
    y_step(3)
    arrived(tall.at[z, c, far, 0], g_s.at[0], g_r.at[0], across)
    arrived(tall.at[z, c, far, 1], g_s.at[2], g_r.at[2], across_pair)
    far_first()
    for load in loads[4:]:
        load.wait()
    copy(fm.at[0], fm.at[1], p_s.at[1], p_r.at[1], pair)
    copy(sm.at[0], sm.at[1], p_s.at[2], p_r.at[2], pair)
    x_step(2, 1)
    x_step(1, 2)
    x_step(3, 1)
    z_step(2)
    x_step(2, 2)
    x_step(1, 3)
    x_step(3, 2)
    z_step(3)
    far_second()
    x_step(2, 3)
    x_step(3, 3)
    z_step(4)
    far_third()
    for d in range(4):
        x_last(d)

    places = ((0, 0), (0, 1), (1, 1), (0, 2), (1, 2), (0, 3), (1, 3), (0, 4))
    for i, (way, s) in enumerate(places):
        for a in (0, 1):
            twin_arrived(a, way, s)
        there = (z + 8 + (-1, 1)[way] * s) % 8
        lhs = jnp.concatenate([wide[there * 4 + k] for k in range(4)], axis=1)
        rhs = jnp.concatenate(
            [
                jnp.concatenate([tall[there, k % 2, k // 2, e] for k in range(4)], axis=0)
                for e in (0, 1)
            ],
            axis=1,
        )
        term = jnp.dot(lhs, rhs, preferred_element_type=F32)
        acc[...] = term if i == 0 else acc[...] + term
    part_out[0] = acc[:, 0:128].astype(BF16)
    part_out[1] = acc[:, 128:256].astype(BF16)
    copy(part_out, part_in, p_s.at[0], p_r.at[0], pair)

    writes = [
        pltpu.make_async_copy(src, dst, w_s.at[i])
        for i, (src, dst) in enumerate(((rot, rot_ref), (near, near_ref), (dist, dist_ref)))
    ]

    def turn(e):
        rotated = acc[:, e * 128 : e * 128 + 128] + part_in[1 - e].astype(F32)
        if e == 0:
            rot[...] = rotated
            writes[0].start()
        new_first = BETA_ONE * fm[e] + (1.0 - BETA_ONE) * rotated
        new_second = BETA_TWO * sm[e] + (1.0 - BETA_TWO) * rotated * rotated
        corr_one = 1.0 - BETA_ONE**STEP
        corr_two = 1.0 - BETA_TWO**STEP
        direction = new_first / corr_one / (jnp.sqrt(new_second / corr_two) + EPSILON)
        turned[e] = direction.T.astype(BF16)

    arrived(fm.at[1], p_s.at[1], p_r.at[1], pair)
    arrived(sm.at[1], p_s.at[2], p_r.at[2], pair)
    arrived(part_in, p_s.at[0], p_r.at[0], pair)

    def terms(e, first, last):
        lhs = turned[e]
        for i in range(first, last):
            base = ((z + 8 + DELTAS[i]) % 8) * 4
            for half in (0, 1):
                rhs = jnp.concatenate([wide[base + half * 2 + c], wide[base + half * 2 + 1 - c]], axis=1)
                term = jnp.dot(lhs, rhs, preferred_element_type=F32)
                own[e, i, half] = term[:, 0:128]
                core_out[e, i, half] = term[:, 128:256].astype(BF16)
            copy(core_out.at[e, i], core_in.at[e, i], tc_s.at[0], tc_r.at[e, i], twin, later=False)

    def from_twin(e, i):
        arrived(core_in.at[e, i], tc_s.at[0], tc_r.at[e, i], twin)

    def stride(e, kind):
        for way in (0, 1):
            to = ((above, below), (above2, below2), (above, below), (above, below))[kind][way]
            i = DELTAS.index(((3, -3), (4, 4), (1, -1), (2, -2))[kind][way])
            if kind == 1:
                total = own[e, i, way] + core_in[e, i, way].astype(F32)
                sent, there = ring_out.at[way, e, 1, way], ring_in.at[way, e, 1, way]
            else:
                total = own[e, i] + core_in[e, i].astype(F32)
                sent, there = ring_out.at[way, e, kind], ring_in.at[way, e, kind]
            if kind == 3:
                arrived(ring_in.at[way, e, 0], r_s.at[0], r_r.at[way, e, 0], to)
                total += ring_in[way, e, 0].astype(F32)
                arrived(ring_in.at[way, e, 1, way], r_s.at[0], r_r.at[way, e, 1], to)
                own[e, i] = total
                own[e, i, way] = own[e, i, way] + ring_in[way, e, 1, way].astype(F32)
                total = own[e, i]
            if kind == 2:
                arrived(ring_in.at[way, e, 3], r_s.at[0], r_r.at[way, e, 3], to)
                total += ring_in[way, e, 3].astype(F32)
            sent[...] = total.astype(BF16)
            copy(sent, there, r_s.at[0], r_r.at[way, e, kind], to, later=False)

    def z_sum(e):
        from_twin(e, HOME)
        total = own[e, HOME] + core_in[e, HOME].astype(F32)
        for way in (0, 1):
            arrived(ring_in.at[way, e, 2], r_s.at[0], r_r.at[way, e, 2], above)
            total += ring_in[way, e, 2].astype(F32)
        own[e, HOME] = total
        last_out[e] = total.astype(BF16)

    turn(0)
    terms(0, 0, 3)
    turn(1)
    terms(1, 0, 3)
    for i in range(3):
        from_twin(0, i)
    stride(0, 0)
    stride(0, 1)
    terms(0, 3, 8)
    for i in range(3):
        from_twin(1, i)
    stride(1, 0)
    stride(1, 1)
    terms(1, 3, 8)
    for i in range(3, 7):
        from_twin(0, i)
    for i in range(3, 7):
        from_twin(1, i)
    stride(0, 3)
    stride(1, 3)
    stride(0, 2)
    stride(1, 2)
    z_sum(0)
    copy(last_out.at[0, far], last_in.at[0], f_s.at[0], f_r.at[0], across)
    z_sum(1)
    copy(last_out.at[1, far], last_in.at[2], f_s.at[2], f_r.at[2], across_pair)
    copy(last_out.at[1, yh], last_in.at[1], f_s.at[1], f_r.at[1], pair)

    pltpu.make_async_copy(wide.at[pl.ds(0, 28)], wide.at[pl.ds(0, 28)], x_s.at[0]).wait()
    pltpu.make_async_copy(tall.at[pl.ds(0, 7), 0], tall.at[pl.ds(0, 7), 0], z_s.at[0]).wait()
    pltpu.make_async_copy(tall.at[:, 0], tall.at[:, 0], gc_s.at[0]).wait()
    pltpu.make_async_copy(core_out, core_out, tc_s.at[0]).wait()
    pltpu.make_async_copy(ring_out.at[:, 1, pl.ds(1, 3)], ring_out.at[:, 1, pl.ds(1, 3)], r_s.at[0]).wait()
    pltpu.make_async_copy(ring_out.at[0], ring_out.at[0], r_s.at[0]).wait()
    for made in waits[:-3]:
        made.wait_send()

    near[mine, :] = own[0, HOME, yh].T
    arrived(last_in.at[1], f_s.at[1], f_r.at[1], pair)
    near[other, :] = last_in[1].astype(F32).T
    writes[1].start()
    arrived(last_in.at[2], f_s.at[2], f_r.at[2], across_pair)
    dist[other, :] = last_in[2].astype(F32).T
    arrived(last_in.at[0], f_s.at[0], f_r.at[0], across)
    dist[mine, :] = last_in[0].astype(F32).T
    writes[2].start()
    for made in waits[-3:]:
        made.wait_send()
    for made in writes:
        made.wait()


def shards(grad, basis_t, first_moment, second_moment, master):
    block = jax.ShapeDtypeStruct(grad.shape, F32)
    dma = pltpu.SemaphoreType.DMA
    rotated, near, dist = pl.pallas_call(
        kernel,
        out_shape=(block, block, block),
        in_specs=[pl.BlockSpec(memory_space=pltpu.HBM)] * 4,
        out_specs=tuple([pl.BlockSpec(memory_space=pltpu.HBM)] * 3),
        scratch_shapes=[
            pltpu.VMEM((2, 256, 128), F32),
            pltpu.VMEM((2, 256, 128), F32),
            pltpu.VMEM((256, 128), F32),
            pltpu.VMEM((256, 128), F32),
            pltpu.VMEM((256, 128), F32),
            pltpu.VMEM((128, 128), BF16),
            pltpu.VMEM((256, 128), BF16),
            pltpu.VMEM((32, 256, 128), BF16),
            pltpu.VMEM((8, 2, 2, 2, 128, 128), BF16),
            pltpu.VMEM((256, 256), F32),
            pltpu.VMEM((2, 256, 128), BF16),
            pltpu.VMEM((2, 256, 128), BF16),
            pltpu.VMEM((2, 128, 256), BF16),
            pltpu.VMEM((2, 8, 2, 128, 128), F32),
            pltpu.VMEM((2, 8, 2, 128, 128), BF16),
            pltpu.VMEM((2, 8, 2, 128, 128), BF16),
            pltpu.VMEM((2, 2, 4, 2, 128, 128), BF16),
            pltpu.VMEM((2, 2, 4, 2, 128, 128), BF16),
            pltpu.VMEM((2, 2, 128, 128), BF16),
            pltpu.VMEM((3, 128, 128), BF16),
            dma((6,)), dma((3,)),
            dma((3,)), dma((3,)),
            dma((1,)), dma((2, 4, 4)),
            dma((3,)), dma((3,)),
            dma((1,)), dma((2, 2, 4)),
            dma((1,)), dma((2, 2, 5)),
            dma((3,)), dma((3,)),
            dma((1,)), dma((2, 8)),
            dma((1,)), dma((2, 2, 4)),
            dma((3,)), dma((3,)),
        ],
        compiler_params=pltpu.CompilerParams(
            collective_id=0, has_side_effects=True, vmem_limit_bytes=60 * 2**20
        ),
        cost_estimate=pl.CostEstimate(flops=2 * 2 * 256 * 8192 * 128, bytes_accessed=2**20, transcendentals=0),
    )(grad, basis_t, first_moment, second_moment)
    new_first = BETA_ONE * first_moment + (1.0 - BETA_ONE) * rotated
    new_second = BETA_TWO * second_moment + (1.0 - BETA_TWO) * rotated * rotated
    rotated_back = near + dist
    new_master = master * (1.0 - LEARN * DECAY) - LEARN * rotated_back
    return (new_first, new_second, new_master, new_master.astype(BF16), rotated_back)


def solution(mesh):
    placed = tuple([P("row", "col")] * 5)
    return jax.shard_map(shards, mesh=mesh, in_specs=placed, out_specs=placed, check_vma=False)
```

```python
import jax
import jax.numpy as jnp
from jax import lax
from jax.experimental import pallas as pl
from jax.experimental.pallas import tpu as pltpu
from jax.sharding import PartitionSpec as P

STEP = 10
BETA_ONE = 0.9
BETA_TWO = 0.95
EPSILON = 1e-08
LEARN = 0.01
DECAY = 0.1

MESH = pl.DeviceIdType.MESH
F32 = jnp.float32
BF16 = jnp.bfloat16

Z_STEPS = (4, 3)
DELTAS = (4, 3, -3, 2, -2, 1, -1, 0)
HOME = DELTAS.index(0)


def kernel(
    g_ref, b_ref, fm_ref, sm_ref,
    rot_ref, near_ref, dist_ref,
    fm, sm, rot, near, dist, give, stage, wide, tall, acc, part_out, part_in, turned,
    own, core_out, core_in, ring_out, ring_in, last_out, last_in,
    l_s, w_s, y_s, y_r, x_s, x_r, g_s, g_r, z_s, z_r, gc_s, gc_r, p_s, p_r, tc_s, tc_r, r_s, r_r, f_s, f_r,
):
    row, col = lax.axis_index("row"), lax.axis_index("col")
    z, yh, c = row // 4, (row // 2) % 2, row % 2
    yl, x = col // 8, col % 8
    h = yl % 2
    mate = yl + 1 - 2 * h
    far = 1 - yh
    here = yl * 8 + x

    def at(z_, yh_, c_, yl_, x_):
        return (z_ * 4 + yh_ * 2 + c_, yl_ * 8 + x_)

    right, left = at(z, yh, c, yl, (x + 1) % 8), at(z, yh, c, yl, (x + 7) % 8)
    right2, left2 = at(z, yh, c, yl, (x + 2) % 8), at(z, yh, c, yl, (x + 6) % 8)
    above, below = at((z + 1) % 8, yh, c, yl, x), at((z + 7) % 8, yh, c, yl, x)
    above2, below2 = at((z + 2) % 8, yh, c, yl, x), at((z + 6) % 8, yh, c, yl, x)
    twin = at(z, yh, 1 - c, yl, x)
    pair = at(z, yh, c, mate, x)
    two_off = at(z, yh, c, (yl + 2) % 4, x)
    mirror = at(z, yh, c, 3 - yl, x)
    across = at(z, far, c, yl, x)
    across_pair = at(z, far, c, mate, x)

    mine = pl.ds(pl.multiple_of(h * 128, 128), 128)
    other = pl.ds(pl.multiple_of((1 - h) * 128, 128), 128)
    loads = [
        pltpu.make_async_copy(src, dst, l_s.at[i])
        for i, (src, dst) in enumerate((
            (b_ref.at[:, mine], wide.at[here]),
            (b_ref.at[:, other], stage),
            (g_ref.at[mine, :], tall.at[z, c, yh, 0]),
            (g_ref.at[other, :], give),
            (fm_ref, fm.at[0]), (sm_ref, sm.at[0]),
        ))
    ]
    for load in loads:
        load.start()
    barrier = pltpu.get_barrier_semaphore()
    peers = [right, left, right2, left2, above, below, above2, below2, twin, pair, two_off, mirror, across, across_pair]
    for peer in peers:
        pl.semaphore_signal(barrier, inc=1, device_id=peer, device_id_type=MESH)

    for load in loads[:4]:
        load.wait()
    pl.semaphore_wait(barrier, len(peers))

    waits = []

    def copy(src, dst, send, recv, to, later=True):
        made = pltpu.make_async_remote_copy(
            src_ref=src, dst_ref=dst, send_sem=send, recv_sem=recv, device_id=to, device_id_type=MESH
        )
        made.start()
        if later:
            waits.append(made)

    def arrived(dst, send, recv, frm):
        pltpu.make_async_remote_copy(
            src_ref=dst, dst_ref=dst, send_sem=send, recv_sem=recv, device_id=frm, device_id_type=MESH
        ).wait_recv()

    inner = ((yl + 1) // 2) % 2
    two, three = (yl + 2) % 4, 3 - yl
    lines = (yl, mate, inner * three + (1 - inner) * two, inner * two + (1 - inner) * three)
    came_by = (None, 0, inner + 1, 2 - inner)

    def x_slot(d, way, s):
        return wide.at[lines[d] * 8 + (x + 8 + (-1, 1)[way] * s) % 8]

    def x_half(d, way):
        return wide.at[lines[d] * 8 + (x + 4) % 8, pl.ds(way * 128, 128)]

    def x_step(d, s):
        for way, to in ((0, right), (1, left)):
            slot = x_slot(d, way, s)
            if s:
                arrived(slot, x_s.at[0], x_r.at[way, d, s - 1], to)
            if s == 3:
                slot = slot.at[pl.ds(way * 128, 128)]
            copy(slot, slot, x_s.at[0], x_r.at[way, d, s], to, later=False)

    def x_first():
        slot = x_slot(0, 0, 0)
        for s, ways in ((0, (right, left)), (1, (right2, left2))):
            for way in (0, 1):
                copy(slot, slot, x_s.at[0], x_r.at[way, 0, s], ways[way], later=False)

    def x_second():
        for way, one, two_on in ((0, right, right2), (1, left, left2)):
            slot = x_slot(0, way, 2)
            arrived(slot, x_s.at[0], x_r.at[way, 0, 1], one)
            copy(slot, slot, x_s.at[0], x_r.at[way, 0, 2], one, later=False)
            part = slot.at[pl.ds(way * 128, 128)]
            copy(part, part, x_s.at[0], x_r.at[way, 0, 3], two_on, later=False)

    def x_last(d):
        for way, one in ((0, right), (1, left)):
            if d == 0:
                arrived(x_slot(0, way, 1), x_s.at[0], x_r.at[way, 0, 0], one)
                arrived(x_slot(0, way, 3), x_s.at[0], x_r.at[way, 0, 2], one)
            arrived(x_half(d, way), x_s.at[0], x_r.at[way, d, 3], one)

    def y_step(d):
        arrived(wide.at[lines[d] * 8 + x], y_s.at[0], y_r.at[came_by[d]], pair)
        x_step(d, 0)

    halves = (yh, far)

    def to_twin(a, way, s):
        sign = (-1, 1)[way]
        slot = tall.at[(z + 8 + sign * s) % 8, c, halves[a]]
        copy(slot, slot, gc_s.at[0], gc_r.at[way, a, s], twin, later=False)

    def twin_arrived(a, way, s):
        sign = (-1, 1)[way]
        slot = tall.at[(z + 8 + sign * s) % 8, 1 - c, halves[a]]
        arrived(slot, gc_s.at[0], gc_r.at[way, a, s], twin)

    def z_step(s):
        for way, sign, to in ((0, -1, above), (1, 1, below)):
            if s > Z_STEPS[way]:
                continue
            slot = tall.at[(z + 8 + sign * s) % 8, c, yh]
            if s:
                arrived(slot, z_s.at[0], z_r.at[way, 0, s - 1], to)
            if s < Z_STEPS[way]:
                copy(slot, slot, z_s.at[0], z_r.at[way, 0, s], to, later=False)
            if s or way == 0:
                to_twin(0, way, s)

    def far_first():
        slot = tall.at[z, c, far]
        for s, ways in ((1, (above2, below2)), (0, (above, below))):
            for way in (0, 1):
                copy(slot, slot, z_s.at[0], z_r.at[way, 1, s], ways[way], later=False)
        to_twin(1, 0, 0)

    def far_second():
        for way, sign, one, two_on in ((0, -1, above, above2), (1, 1, below, below2)):
            slot = tall.at[(z + 8 + sign * 2) % 8, c, far]
            arrived(slot, z_s.at[0], z_r.at[way, 1, 1], one)
            copy(slot.at[way], slot.at[way], z_s.at[0], z_r.at[way, 1, 3], two_on, later=False)
            copy(slot, slot, z_s.at[0], z_r.at[way, 1, 2], one, later=False)
        for s in (2, 1):
            for way, sign, one in ((0, -1, above), (1, 1, below)):
                if s == 1:
                    arrived(tall.at[(z + 8 + sign) % 8, c, far], z_s.at[0], z_r.at[way, 1, 0], one)
                to_twin(1, way, s)

    def far_third():
        for way, sign, one in ((0, -1, above), (1, 1, below)):
            arrived(tall.at[(z + 8 + sign * 3) % 8, c, far], z_s.at[0], z_r.at[way, 1, 2], one)
            to_twin(1, way, 3)
        for way, one in ((0, above), (1, below)):
            arrived(tall.at[(z + 4) % 8, c, far, way], z_s.at[0], z_r.at[way, 1, 3], one)
        to_twin(1, 0, 4)

    x_first()
    copy(give, tall.at[z, c, yh, 1], g_s.at[1], g_r.at[1], pair)
    copy(stage, wide.at[here], y_s.at[0], y_r.at[0], pair)
    copy(stage, wide.at[here], y_s.at[2], y_r.at[2], mirror)
    copy(wide.at[here], wide.at[here], y_s.at[1], y_r.at[1], two_off)

    arrived(tall.at[z, c, yh, 1], g_s.at[1], g_r.at[1], pair)
    z_step(0)
    copy(tall.at[z, c, yh, 0], tall.at[z, c, yh, 0], g_s.at[0], g_r.at[0], across)
    copy(give, tall.at[z, c, yh, 1], g_s.at[2], g_r.at[2], across_pair)
    y_step(1)
    x_second()
    y_step(2)
    z_step(1)
    x_step(1, 1)
    y_step(3)
    arrived(tall.at[z, c, far, 0], g_s.at[0], g_r.at[0], across)
    arrived(tall.at[z, c, far, 1], g_s.at[2], g_r.at[2], across_pair)
    far_first()
    for load in loads[4:]:
        load.wait()
    copy(fm.at[0], fm.at[1], p_s.at[1], p_r.at[1], pair)
    copy(sm.at[0], sm.at[1], p_s.at[2], p_r.at[2], pair)
    x_step(2, 1)
    z_step(2)
    x_step(1, 2)
    x_step(3, 1)
    x_step(2, 2)
    far_second()
    z_step(3)
    x_step(1, 3)
    x_step(3, 2)
    x_step(2, 3)
    z_step(4)
    far_third()
    x_step(3, 3)
    x_last(0)
    for s in range(5):
        for a in (0, 1):
            for way in (0, 1):
                if way == 0 or s in (1, 2, 3):
                    twin_arrived(a, way, s)

    for delta in (0, 1, -1, 2, -2, 3, -3, 4):
        if delta == 4:
            for d in (1, 2, 3):
                x_last(d)
        there = (x + 8 + delta) % 8
        lhs = jnp.concatenate([wide[line * 8 + there] for line in range(4)], axis=1)
        rhs = jnp.concatenate(
            [
                jnp.concatenate(
                    [tall[line * 2 + there // 4, there % 2, (there // 2) % 2, e] for line in range(4)],
                    axis=0,
                )
                for e in (0, 1)
            ],
            axis=1,
        )
        term = jnp.dot(lhs, rhs, preferred_element_type=F32)
        acc[...] = term if delta == 0 else acc[...] + term
    part_out[0] = acc[:, 0:128].astype(BF16)
    copy(part_out.at[0], part_in.at[0], p_s.at[0], p_r.at[0], pair)
    part_out[1] = acc[:, 128:256].astype(BF16)
    copy(part_out.at[1], part_in.at[1], p_s.at[3], p_r.at[3], pair)

    writes = [
        pltpu.make_async_copy(src, dst, w_s.at[i])
        for i, (src, dst) in enumerate(((rot, rot_ref), (near, near_ref), (dist, dist_ref)))
    ]

    def turn(e):
        rotated = acc[:, e * 128 : e * 128 + 128] + part_in[1 - e].astype(F32)
        if e == 0:
            rot[...] = rotated
            writes[0].start()
        new_first = BETA_ONE * fm[e] + (1.0 - BETA_ONE) * rotated
        new_second = BETA_TWO * sm[e] + (1.0 - BETA_TWO) * rotated * rotated
        corr_one = 1.0 - BETA_ONE**STEP
        corr_two = 1.0 - BETA_TWO**STEP
        direction = new_first / corr_one / (jnp.sqrt(new_second / corr_two) + EPSILON)
        turned[e] = direction.T.astype(BF16)

    arrived(fm.at[1], p_s.at[1], p_r.at[1], pair)
    arrived(sm.at[1], p_s.at[2], p_r.at[2], pair)
    arrived(part_in.at[0], p_s.at[0], p_r.at[0], pair)

    def terms(e, first, last):
        lhs = turned[e]
        for i in range(first, last):
            base = ((z + 8 + DELTAS[i]) % 8) * 4
            for half in (0, 1):
                rhs = jnp.concatenate([wide[base + half * 2 + c], wide[base + half * 2 + 1 - c]], axis=1)
                term = jnp.dot(lhs, rhs, preferred_element_type=F32)
                own[e, i, half] = term[:, 0:128]
                core_out[e, i, half] = term[:, 128:256].astype(BF16)
            copy(core_out.at[e, i], core_in.at[e, i], tc_s.at[0], tc_r.at[e, i], twin, later=False)

    def from_twin(e, i):
        arrived(core_in.at[e, i], tc_s.at[0], tc_r.at[e, i], twin)

    def stride(e, kind):
        for way in (0, 1):
            to = ((above, below), (above2, below2), (above, below), (above, below))[kind][way]
            i = DELTAS.index(((3, -3), (4, 4), (1, -1), (2, -2))[kind][way])
            if kind == 1:
                total = own[e, i, way] + core_in[e, i, way].astype(F32)
                sent, there = ring_out.at[way, e, 1, way], ring_in.at[way, e, 1, way]
            else:
                total = own[e, i] + core_in[e, i].astype(F32)
                sent, there = ring_out.at[way, e, kind], ring_in.at[way, e, kind]
            if kind == 3:
                arrived(ring_in.at[way, e, 0], r_s.at[0], r_r.at[way, e, 0], to)
                total += ring_in[way, e, 0].astype(F32)
                arrived(ring_in.at[way, e, 1, way], r_s.at[0], r_r.at[way, e, 1], to)
                own[e, i] = total
                own[e, i, way] = own[e, i, way] + ring_in[way, e, 1, way].astype(F32)
                total = own[e, i]
            if kind == 2:
                arrived(ring_in.at[way, e, 3], r_s.at[0], r_r.at[way, e, 3], to)
                total += ring_in[way, e, 3].astype(F32)
            sent[...] = total.astype(BF16)
            copy(sent, there, r_s.at[0], r_r.at[way, e, kind], to, later=False)

    def z_sum(e):
        from_twin(e, HOME)
        total = own[e, HOME] + core_in[e, HOME].astype(F32)
        for way in (0, 1):
            arrived(ring_in.at[way, e, 2], r_s.at[0], r_r.at[way, e, 2], above)
            total += ring_in[way, e, 2].astype(F32)
        own[e, HOME] = total
        last_out[e] = total.astype(BF16)

    turn(1)
    terms(1, 0, 3)
    arrived(part_in.at[1], p_s.at[3], p_r.at[3], pair)
    turn(0)
    terms(0, 0, 3)
    for i in range(3):
        from_twin(1, i)
    stride(1, 0)
    stride(1, 1)
    terms(1, 3, 8)
    for i in range(3):
        from_twin(0, i)
    stride(0, 0)
    stride(0, 1)
    terms(0, 3, 8)
    for i in range(3, 7):
        from_twin(1, i)
    for i in range(3, 7):
        from_twin(0, i)
    stride(1, 3)
    stride(0, 3)
    stride(1, 2)
    stride(0, 2)
    z_sum(1)
    copy(last_out.at[1, far], last_in.at[2], f_s.at[2], f_r.at[2], across_pair)
    copy(last_out.at[1, yh], last_in.at[1], f_s.at[1], f_r.at[1], pair)
    z_sum(0)
    copy(last_out.at[0, far], last_in.at[0], f_s.at[0], f_r.at[0], across)

    pltpu.make_async_copy(wide.at[pl.ds(0, 28)], wide.at[pl.ds(0, 28)], x_s.at[0]).wait()
    pltpu.make_async_copy(tall.at[pl.ds(0, 7), 0], tall.at[pl.ds(0, 7), 0], z_s.at[0]).wait()
    pltpu.make_async_copy(tall.at[:, 0], tall.at[:, 0], gc_s.at[0]).wait()
    pltpu.make_async_copy(core_out, core_out, tc_s.at[0]).wait()
    pltpu.make_async_copy(ring_out.at[:, 1, pl.ds(1, 3)], ring_out.at[:, 1, pl.ds(1, 3)], r_s.at[0]).wait()
    pltpu.make_async_copy(ring_out.at[0], ring_out.at[0], r_s.at[0]).wait()
    for made in waits[:-3]:
        made.wait_send()

    near[mine, :] = own[0, HOME, yh].T
    arrived(last_in.at[1], f_s.at[1], f_r.at[1], pair)
    near[other, :] = last_in[1].astype(F32).T
    writes[1].start()
    arrived(last_in.at[2], f_s.at[2], f_r.at[2], across_pair)
    dist[other, :] = last_in[2].astype(F32).T
    arrived(last_in.at[0], f_s.at[0], f_r.at[0], across)
    dist[mine, :] = last_in[0].astype(F32).T
    writes[2].start()
    for made in waits[-3:]:
        made.wait_send()
    for made in writes:
        made.wait()


def shards(grad, basis_t, first_moment, second_moment, master):
    block = jax.ShapeDtypeStruct(grad.shape, F32)
    dma = pltpu.SemaphoreType.DMA
    rotated, near, dist = pl.pallas_call(
        kernel,
        out_shape=(block, block, block),
        in_specs=[pl.BlockSpec(memory_space=pltpu.HBM)] * 4,
        out_specs=tuple([pl.BlockSpec(memory_space=pltpu.HBM)] * 3),
        scratch_shapes=[
            pltpu.VMEM((2, 256, 128), F32),
            pltpu.VMEM((2, 256, 128), F32),
            pltpu.VMEM((256, 128), F32),
            pltpu.VMEM((256, 128), F32),
            pltpu.VMEM((256, 128), F32),
            pltpu.VMEM((128, 128), BF16),
            pltpu.VMEM((256, 128), BF16),
            pltpu.VMEM((32, 256, 128), BF16),
            pltpu.VMEM((8, 2, 2, 2, 128, 128), BF16),
            pltpu.VMEM((256, 256), F32),
            pltpu.VMEM((2, 256, 128), BF16),
            pltpu.VMEM((2, 256, 128), BF16),
            pltpu.VMEM((2, 128, 256), BF16),
            pltpu.VMEM((2, 8, 2, 128, 128), F32),
            pltpu.VMEM((2, 8, 2, 128, 128), BF16),
            pltpu.VMEM((2, 8, 2, 128, 128), BF16),
            pltpu.VMEM((2, 2, 4, 2, 128, 128), BF16),
            pltpu.VMEM((2, 2, 4, 2, 128, 128), BF16),
            pltpu.VMEM((2, 2, 128, 128), BF16),
            pltpu.VMEM((3, 128, 128), BF16),
            dma((6,)), dma((3,)),
            dma((3,)), dma((3,)),
            dma((1,)), dma((2, 4, 4)),
            dma((3,)), dma((3,)),
            dma((1,)), dma((2, 2, 4)),
            dma((1,)), dma((2, 2, 5)),
            dma((4,)), dma((4,)),
            dma((1,)), dma((2, 8)),
            dma((1,)), dma((2, 2, 4)),
            dma((3,)), dma((3,)),
        ],
        compiler_params=pltpu.CompilerParams(
            collective_id=0, has_side_effects=True, vmem_limit_bytes=60 * 2**20
        ),
        cost_estimate=pl.CostEstimate(flops=2 * 2 * 256 * 8192 * 128, bytes_accessed=2**20, transcendentals=0),
    )(grad, basis_t, first_moment, second_moment)
    new_first = BETA_ONE * first_moment + (1.0 - BETA_ONE) * rotated
    new_second = BETA_TWO * second_moment + (1.0 - BETA_TWO) * rotated * rotated
    rotated_back = near + dist
    new_master = master * (1.0 - LEARN * DECAY) - LEARN * rotated_back
    return (new_first, new_second, new_master, new_master.astype(BF16), rotated_back)


def solution(mesh):
    placed = tuple([P("row", "col")] * 5)
    return jax.shard_map(shards, mesh=mesh, in_specs=placed, out_specs=placed, check_vma=False)
```

```python
import jax
import jax.numpy as jnp
from jax import lax
from jax.experimental import pallas as pl
from jax.experimental.pallas import tpu as pltpu
from jax.sharding import PartitionSpec as P

STEP = 10
BETA_ONE = 0.9
BETA_TWO = 0.95
EPSILON = 1e-08
LEARN = 0.01
DECAY = 0.1

MESH = pl.DeviceIdType.MESH
F32 = jnp.float32
BF16 = jnp.bfloat16

Z_STEPS = (4, 3)
DELTAS = (4, 3, -3, 2, -2, 1, -1, 0)
HOME = DELTAS.index(0)


def kernel(
    g_ref, b_ref, fm_ref, sm_ref,
    rot_ref, near_ref, dist_ref,
    fm, sm, rot, near, dist, give, stage, wide, tall, acc, part_out, part_in, turned,
    own, core_out, core_in, ring_out, ring_in, last_out, last_in,
    l_s, w_s, y_s, y_r, x_s, x_r, g_s, g_r, z_s, z_r, gc_s, gc_r, p_s, p_r, tc_s, tc_r, r_s, r_r, f_s, f_r,
):
    row, col = lax.axis_index("row"), lax.axis_index("col")
    z, yh, c = row // 4, (row // 2) % 2, row % 2
    yl, x = col // 8, col % 8
    h = yl % 2
    mate = yl + 1 - 2 * h
    far = 1 - yh
    here = yl * 8 + x

    def at(z_, yh_, c_, yl_, x_):
        return (z_ * 4 + yh_ * 2 + c_, yl_ * 8 + x_)

    right, left = at(z, yh, c, yl, (x + 1) % 8), at(z, yh, c, yl, (x + 7) % 8)
    right2, left2 = at(z, yh, c, yl, (x + 2) % 8), at(z, yh, c, yl, (x + 6) % 8)
    above, below = at((z + 1) % 8, yh, c, yl, x), at((z + 7) % 8, yh, c, yl, x)
    above2, below2 = at((z + 2) % 8, yh, c, yl, x), at((z + 6) % 8, yh, c, yl, x)
    twin = at(z, yh, 1 - c, yl, x)
    pair = at(z, yh, c, mate, x)
    two_off = at(z, yh, c, (yl + 2) % 4, x)
    mirror = at(z, yh, c, 3 - yl, x)
    across = at(z, far, c, yl, x)
    across_pair = at(z, far, c, mate, x)

    mine = pl.ds(pl.multiple_of(h * 128, 128), 128)
    other = pl.ds(pl.multiple_of((1 - h) * 128, 128), 128)
    loads = [
        pltpu.make_async_copy(src, dst, l_s.at[i])
        for i, (src, dst) in enumerate((
            (b_ref.at[:, mine], wide.at[here]),
            (b_ref.at[:, other], stage),
            (g_ref.at[mine, :], tall.at[z, c, yh, 0]),
            (g_ref.at[other, :], give),
            (fm_ref, fm.at[0]), (sm_ref, sm.at[0]),
        ))
    ]
    for load in loads:
        load.start()
    barrier = pltpu.get_barrier_semaphore()
    peers = [right, left, right2, left2, above, below, above2, below2, twin, pair, two_off, mirror, across, across_pair]
    for peer in peers:
        pl.semaphore_signal(barrier, inc=1, device_id=peer, device_id_type=MESH)

    for load in loads[:4]:
        load.wait()
    pl.semaphore_wait(barrier, len(peers))

    waits = []

    def copy(src, dst, send, recv, to, later=True):
        made = pltpu.make_async_remote_copy(
            src_ref=src, dst_ref=dst, send_sem=send, recv_sem=recv, device_id=to, device_id_type=MESH
        )
        made.start()
        if later:
            waits.append(made)

    def arrived(dst, send, recv, frm):
        pltpu.make_async_remote_copy(
            src_ref=dst, dst_ref=dst, send_sem=send, recv_sem=recv, device_id=frm, device_id_type=MESH
        ).wait_recv()

    inner = ((yl + 1) // 2) % 2
    two, three = (yl + 2) % 4, 3 - yl
    lines = (yl, mate, inner * three + (1 - inner) * two, inner * two + (1 - inner) * three)
    came_by = (None, 0, inner + 1, 2 - inner)

    def x_slot(d, way, s):
        return wide.at[lines[d] * 8 + (x + 8 + (-1, 1)[way] * s) % 8]

    def x_half(d, way):
        return wide.at[lines[d] * 8 + (x + 4) % 8, pl.ds(way * 128, 128)]

    def x_step(d, s):
        for way, to in ((0, right), (1, left)):
            slot = x_slot(d, way, s)
            if s:
                arrived(slot, x_s.at[0], x_r.at[way, d, s - 1], to)
            if s == 3:
                slot = slot.at[pl.ds(way * 128, 128)]
            copy(slot, slot, x_s.at[0], x_r.at[way, d, s], to, later=False)

    def x_first():
        slot = x_slot(0, 0, 0)
        for s, ways in ((0, (right, left)), (1, (right2, left2))):
            for way in (0, 1):
                copy(slot, slot, x_s.at[0], x_r.at[way, 0, s], ways[way], later=False)

    def x_second():
        for way, one, two_on in ((0, right, right2), (1, left, left2)):
            slot = x_slot(0, way, 2)
            arrived(slot, x_s.at[0], x_r.at[way, 0, 1], one)
            copy(slot, slot, x_s.at[0], x_r.at[way, 0, 2], one, later=False)
            part = slot.at[pl.ds(way * 128, 128)]
            copy(part, part, x_s.at[0], x_r.at[way, 0, 3], two_on, later=False)

    def x_last(d):
        for way, one in ((0, right), (1, left)):
            if d == 0:
                arrived(x_slot(0, way, 1), x_s.at[0], x_r.at[way, 0, 0], one)
                arrived(x_slot(0, way, 3), x_s.at[0], x_r.at[way, 0, 2], one)
            arrived(x_half(d, way), x_s.at[0], x_r.at[way, d, 3], one)

    def y_step(d):
        arrived(wide.at[lines[d] * 8 + x], y_s.at[0], y_r.at[came_by[d]], pair)
        x_step(d, 0)

    halves = (yh, far)

    def to_twin(a, way, s):
        sign = (-1, 1)[way]
        slot = tall.at[(z + 8 + sign * s) % 8, c, halves[a]]
        copy(slot, slot, gc_s.at[0], gc_r.at[way, a, s], twin, later=False)

    def twin_arrived(a, way, s):
        sign = (-1, 1)[way]
        slot = tall.at[(z + 8 + sign * s) % 8, 1 - c, halves[a]]
        arrived(slot, gc_s.at[0], gc_r.at[way, a, s], twin)

    def z_step(s):
        for way, sign, to in ((0, -1, above), (1, 1, below)):
            if s > Z_STEPS[way]:
                continue
            slot = tall.at[(z + 8 + sign * s) % 8, c, yh]
            if s:
                arrived(slot, z_s.at[0], z_r.at[way, 0, s - 1], to)
            if s < Z_STEPS[way]:
                copy(slot, slot, z_s.at[0], z_r.at[way, 0, s], to, later=False)
            if s or way == 0:
                to_twin(0, way, s)

    def far_first():
        slot = tall.at[z, c, far]
        for s, ways in ((1, (above2, below2)), (0, (above, below))):
            for way in (0, 1):
                copy(slot, slot, z_s.at[0], z_r.at[way, 1, s], ways[way], later=False)
        to_twin(1, 0, 0)

    def far_second():
        for way, sign, one, two_on in ((0, -1, above, above2), (1, 1, below, below2)):
            slot = tall.at[(z + 8 + sign * 2) % 8, c, far]
            arrived(slot, z_s.at[0], z_r.at[way, 1, 1], one)
            copy(slot.at[way], slot.at[way], z_s.at[0], z_r.at[way, 1, 3], two_on, later=False)
            copy(slot, slot, z_s.at[0], z_r.at[way, 1, 2], one, later=False)
        for s in (2, 1):
            for way, sign, one in ((0, -1, above), (1, 1, below)):
                if s == 1:
                    arrived(tall.at[(z + 8 + sign) % 8, c, far], z_s.at[0], z_r.at[way, 1, 0], one)
                to_twin(1, way, s)

    def far_third():
        for way, sign, one in ((0, -1, above), (1, 1, below)):
            arrived(tall.at[(z + 8 + sign * 3) % 8, c, far], z_s.at[0], z_r.at[way, 1, 2], one)
            to_twin(1, way, 3)
        for way, one in ((0, above), (1, below)):
            arrived(tall.at[(z + 4) % 8, c, far, way], z_s.at[0], z_r.at[way, 1, 3], one)
        to_twin(1, 0, 4)

    x_first()
    copy(give, tall.at[z, c, yh, 1], g_s.at[1], g_r.at[1], pair)
    copy(stage, wide.at[here], y_s.at[0], y_r.at[0], pair)
    copy(stage, wide.at[here], y_s.at[2], y_r.at[2], mirror)
    copy(wide.at[here], wide.at[here], y_s.at[1], y_r.at[1], two_off)

    arrived(tall.at[z, c, yh, 1], g_s.at[1], g_r.at[1], pair)
    z_step(0)
    copy(tall.at[z, c, yh, 0], tall.at[z, c, yh, 0], g_s.at[0], g_r.at[0], across)
    copy(give, tall.at[z, c, yh, 1], g_s.at[2], g_r.at[2], across_pair)
    y_step(1)
    x_second()
    y_step(2)
    z_step(1)
    x_step(1, 1)
    y_step(3)
    arrived(tall.at[z, c, far, 0], g_s.at[0], g_r.at[0], across)
    arrived(tall.at[z, c, far, 1], g_s.at[2], g_r.at[2], across_pair)
    far_first()
    for load in loads[4:]:
        load.wait()
    copy(fm.at[0], fm.at[1], p_s.at[1], p_r.at[1], pair)
    copy(sm.at[0], sm.at[1], p_s.at[2], p_r.at[2], pair)
    x_step(2, 1)
    z_step(2)
    x_step(1, 2)
    x_step(3, 1)
    x_step(2, 2)
    far_second()
    z_step(3)
    x_step(1, 3)
    x_step(3, 2)
    x_step(2, 3)
    z_step(4)
    far_third()
    x_step(3, 3)
    x_last(0)
    for s in range(5):
        for a in (0, 1):
            for way in (0, 1):
                if way == 0 or s in (1, 2, 3):
                    twin_arrived(a, way, s)

    for delta in (0, 1, -1, 2, -2, 3, -3, 4):
        if delta == 4:
            for d in (1, 2, 3):
                x_last(d)
        there = (x + 8 + delta) % 8
        lhs = jnp.concatenate([wide[line * 8 + there] for line in range(4)], axis=1)
        rhs = jnp.concatenate(
            [
                jnp.concatenate(
                    [tall[line * 2 + there // 4, there % 2, (there // 2) % 2, e] for line in range(4)],
                    axis=0,
                )
                for e in (0, 1)
            ],
            axis=1,
        )
        term = jnp.dot(lhs, rhs, preferred_element_type=F32)
        acc[...] = term if delta == 0 else acc[...] + term
    part_out[0] = acc[:, 0:128].astype(BF16)
    copy(part_out.at[0], part_in.at[0], p_s.at[0], p_r.at[0], pair)
    part_out[1] = acc[:, 128:256].astype(BF16)
    copy(part_out.at[1], part_in.at[1], p_s.at[3], p_r.at[3], pair)

    writes = [
        pltpu.make_async_copy(src, dst, w_s.at[i])
        for i, (src, dst) in enumerate(((rot, rot_ref), (near, near_ref), (dist, dist_ref)))
    ]

    def turn(e):
        rotated = acc[:, e * 128 : e * 128 + 128] + part_in[1 - e].astype(F32)
        if e == 0:
            rot[...] = rotated
            writes[0].start()
        new_first = BETA_ONE * fm[e] + (1.0 - BETA_ONE) * rotated
        new_second = BETA_TWO * sm[e] + (1.0 - BETA_TWO) * rotated * rotated
        corr_one = 1.0 - BETA_ONE**STEP
        corr_two = 1.0 - BETA_TWO**STEP
        direction = new_first / corr_one / (jnp.sqrt(new_second / corr_two) + EPSILON)
        turned[e] = direction.T.astype(BF16)

    arrived(fm.at[1], p_s.at[1], p_r.at[1], pair)
    arrived(sm.at[1], p_s.at[2], p_r.at[2], pair)
    arrived(part_in.at[0], p_s.at[0], p_r.at[0], pair)

    def terms(e, first, last):
        lhs = turned[e]
        for i in range(first, last):
            base = ((z + 8 + DELTAS[i]) % 8) * 4
            for half in (0, 1):
                rhs = jnp.concatenate([wide[base + half * 2 + c], wide[base + half * 2 + 1 - c]], axis=1)
                term = jnp.dot(lhs, rhs, preferred_element_type=F32)
                own[e, i, half] = term[:, 0:128]
                core_out[e, i, half] = term[:, 128:256].astype(BF16)
            copy(core_out.at[e, i], core_in.at[e, i], tc_s.at[0], tc_r.at[e, i], twin, later=False)

    def from_twin(e, i):
        arrived(core_in.at[e, i], tc_s.at[0], tc_r.at[e, i], twin)

    def stride(e, kind):
        for way in (0, 1):
            to = ((above, below), (above2, below2), (above, below), (above, below))[kind][way]
            i = DELTAS.index(((3, -3), (4, 4), (1, -1), (2, -2))[kind][way])
            if kind == 1:
                total = own[e, i, way] + core_in[e, i, way].astype(F32)
                sent, there = ring_out.at[way, e, 1, way], ring_in.at[way, e, 1, way]
            else:
                total = own[e, i] + core_in[e, i].astype(F32)
                sent, there = ring_out.at[way, e, kind], ring_in.at[way, e, kind]
            if kind == 3:
                arrived(ring_in.at[way, e, 0], r_s.at[0], r_r.at[way, e, 0], to)
                total += ring_in[way, e, 0].astype(F32)
                arrived(ring_in.at[way, e, 1, way], r_s.at[0], r_r.at[way, e, 1], to)
                own[e, i] = total
                own[e, i, way] = own[e, i, way] + ring_in[way, e, 1, way].astype(F32)
                total = own[e, i]
            if kind == 2:
                arrived(ring_in.at[way, e, 3], r_s.at[0], r_r.at[way, e, 3], to)
                total += ring_in[way, e, 3].astype(F32)
            sent[...] = total.astype(BF16)
            copy(sent, there, r_s.at[0], r_r.at[way, e, kind], to, later=False)

    def z_sum(e):
        from_twin(e, HOME)
        total = own[e, HOME] + core_in[e, HOME].astype(F32)
        for way in (0, 1):
            arrived(ring_in.at[way, e, 2], r_s.at[0], r_r.at[way, e, 2], above)
            total += ring_in[way, e, 2].astype(F32)
        own[e, HOME] = total
        last_out[e] = total.astype(BF16)

    turn(1)
    terms(1, 0, 3)
    arrived(part_in.at[1], p_s.at[3], p_r.at[3], pair)
    turn(0)
    terms(0, 0, 3)
    for i in range(3):
        from_twin(1, i)
    stride(1, 0)
    stride(1, 1)
    terms(1, 3, 8)
    for i in range(3):
        from_twin(0, i)
    stride(0, 0)
    stride(0, 1)
    terms(0, 3, 8)
    for i in range(3, 7):
        from_twin(1, i)
    for i in range(3, 7):
        from_twin(0, i)
    stride(1, 3)
    stride(0, 3)
    stride(1, 2)
    stride(0, 2)
    z_sum(1)
    copy(last_out.at[1, far], last_in.at[2], f_s.at[2], f_r.at[2], across_pair)
    copy(last_out.at[1, yh], last_in.at[1], f_s.at[1], f_r.at[1], pair)
    z_sum(0)
    copy(last_out.at[0, far], last_in.at[0], f_s.at[0], f_r.at[0], across)

    pltpu.make_async_copy(wide.at[pl.ds(0, 28)], wide.at[pl.ds(0, 28)], x_s.at[0]).wait()
    pltpu.make_async_copy(tall.at[pl.ds(0, 7), 0], tall.at[pl.ds(0, 7), 0], z_s.at[0]).wait()
    pltpu.make_async_copy(tall.at[:, 0], tall.at[:, 0], gc_s.at[0]).wait()
    pltpu.make_async_copy(core_out, core_out, tc_s.at[0]).wait()
    pltpu.make_async_copy(ring_out.at[:, 1, pl.ds(1, 3)], ring_out.at[:, 1, pl.ds(1, 3)], r_s.at[0]).wait()
    pltpu.make_async_copy(ring_out.at[0], ring_out.at[0], r_s.at[0]).wait()
    for made in waits[:-3]:
        made.wait_send()

    near[mine, :] = own[0, HOME, yh].T
    arrived(last_in.at[1], f_s.at[1], f_r.at[1], pair)
    near[other, :] = last_in[1].astype(F32).T
    writes[1].start()
    arrived(last_in.at[2], f_s.at[2], f_r.at[2], across_pair)
    dist[other, :] = last_in[2].astype(F32).T.astype(BF16)
    arrived(last_in.at[0], f_s.at[0], f_r.at[0], across)
    dist[mine, :] = last_in[0].astype(F32).T.astype(BF16)
    writes[2].start()
    for made in waits[-3:]:
        made.wait_send()
    for made in writes:
        made.wait()


def shards(grad, basis_t, first_moment, second_moment, master):
    block = jax.ShapeDtypeStruct(grad.shape, F32)
    dma = pltpu.SemaphoreType.DMA
    rotated, near, dist = pl.pallas_call(
        kernel,
        out_shape=(block, block, jax.ShapeDtypeStruct(grad.shape, BF16)),
        in_specs=[pl.BlockSpec(memory_space=pltpu.HBM)] * 4,
        out_specs=tuple([pl.BlockSpec(memory_space=pltpu.HBM)] * 3),
        scratch_shapes=[
            pltpu.VMEM((2, 256, 128), F32),
            pltpu.VMEM((2, 256, 128), F32),
            pltpu.VMEM((256, 128), F32),
            pltpu.VMEM((256, 128), F32),
            pltpu.VMEM((256, 128), BF16),
            pltpu.VMEM((128, 128), BF16),
            pltpu.VMEM((256, 128), BF16),
            pltpu.VMEM((32, 256, 128), BF16),
            pltpu.VMEM((8, 2, 2, 2, 128, 128), BF16),
            pltpu.VMEM((256, 256), F32),
            pltpu.VMEM((2, 256, 128), BF16),
            pltpu.VMEM((2, 256, 128), BF16),
            pltpu.VMEM((2, 128, 256), BF16),
            pltpu.VMEM((2, 8, 2, 128, 128), F32),
            pltpu.VMEM((2, 8, 2, 128, 128), BF16),
            pltpu.VMEM((2, 8, 2, 128, 128), BF16),
            pltpu.VMEM((2, 2, 4, 2, 128, 128), BF16),
            pltpu.VMEM((2, 2, 4, 2, 128, 128), BF16),
            pltpu.VMEM((2, 2, 128, 128), BF16),
            pltpu.VMEM((3, 128, 128), BF16),
            dma((6,)), dma((3,)),
            dma((3,)), dma((3,)),
            dma((1,)), dma((2, 4, 4)),
            dma((3,)), dma((3,)),
            dma((1,)), dma((2, 2, 4)),
            dma((1,)), dma((2, 2, 5)),
            dma((4,)), dma((4,)),
            dma((1,)), dma((2, 8)),
            dma((1,)), dma((2, 2, 4)),
            dma((3,)), dma((3,)),
        ],
        compiler_params=pltpu.CompilerParams(
            collective_id=0, has_side_effects=True, vmem_limit_bytes=60 * 2**20
        ),
        cost_estimate=pl.CostEstimate(flops=2 * 2 * 256 * 8192 * 128, bytes_accessed=2**20, transcendentals=0),
    )(grad, basis_t, first_moment, second_moment)
    new_first = BETA_ONE * first_moment + (1.0 - BETA_ONE) * rotated
    new_second = BETA_TWO * second_moment + (1.0 - BETA_TWO) * rotated * rotated
    rotated_back = near + dist.astype(F32)
    new_master = master * (1.0 - LEARN * DECAY) - LEARN * rotated_back
    return (new_first, new_second, new_master, new_master.astype(BF16), rotated_back)


def solution(mesh):
    placed = tuple([P("row", "col")] * 5)
    return jax.shard_map(shards, mesh=mesh, in_specs=placed, out_specs=placed, check_vma=False)
```
